256 devices in a mesh: seq: 32 (over x_hi, z, core), head: 8 (over y, x_lo).
Axes of the slice: x: 4 (x_hi: 2, x_lo: 2; x = x_hi * 2 + x_lo), y: 4, z: 8, core: 2. Of those that a mesh axis runs over, the one named last changes fastest.
Arguments:
- prompt_queries: bfloat16 [4096, 1024], P('seq', 'head'), may hold values from -130 to 130
- prompt_cache: bfloat16 [4096, 256], P('seq'), may hold values from -7 to 7
- response_queries: bfloat16 [32768, 1024], P('seq', 'head'), may hold values from -130 to 130
- response_cache: bfloat16 [32768, 256], P('seq'), may hold values from -6 to 6
- prompt_cotangent: bfloat16 [4096, 1024], P('seq', 'head'), may hold values from -6 to 6
- response_cotangent: bfloat16 [32768, 1024], P('seq', 'head'), may hold values from -6 to 6
- response_lengths: int32 [32], P('seq'), may hold values from 0 to 1024, as said below
Outputs:
- prompt_output: bfloat16 [4096, 1024], P('seq', 'head')
- response_output: bfloat16 [32768, 1024], P('seq', 'head')
- prompt_adjoint: bfloat16 [4096, 1024], P('seq', 'head')
- response_adjoint: bfloat16 [32768, 1024], P('seq', 'head')
- prompt_cachegrad: bfloat16 [4096, 256], P('seq')
- response_cachegrad: bfloat16 [32768, 256], P('seq')
The draws below stay inside these ranges and needn't reach their ends.
Inputs may be any that keep to these rules, and one draw needn't show every extreme that they name: `response_lengths`: 16 slots are non-empty; a non-empty slot holds 512 or more tokens; in every draw some slot holds 1024 tokens.
All inputs are finite; a program needn't handle non-finite values.
Results may differ from the reference program's by a relative error of at most 0.011.
Values may be sent and summed in bfloat16 or wider, within the bound.
No kernel may reach another device: no remote copies, remote signals or barrier semaphores. Data moves between devices by JAX's collectives and lax.ppermute only.
A program may use at most 128 MiB of HBM per device.

```python
import math
import jax
import jax.numpy as jnp
from jax import lax

HD = 128
QH = 8
RLEN = 1024
PROMPT = 4096
RESP = 16
SLOTS = 32
RROWS = 32768


def prompt_keys_base(key):
    drawn = jax.random.normal(jax.random.fold_in(key, 11), (PROMPT, HD), jnp.float32)
    return jnp.clip(drawn, -6.0, 6.0)


def draw_prompt_cache(key, part):
    keys = prompt_keys_base(key)
    key = jax.random.fold_in(key, 1)
    values = jnp.clip(jax.random.normal(key, (PROMPT, HD), jnp.float32), -6.0, 6.0)
    return jnp.concatenate([keys, values], axis=1).astype(jnp.bfloat16)


def draw_prompt_queries(key, part):
    key = jax.random.fold_in(key, 2)
    queries = jnp.clip(jax.random.normal(key, (PROMPT, QH * HD), jnp.float32), -6.0, 6.0)
    return queries.astype(jnp.bfloat16)


def draw_response_queries(key, part):
    key = jax.random.fold_in(key, 3)
    queries = jnp.clip(jax.random.normal(key, (RROWS, QH * HD), jnp.float32), -6.0, 6.0)
    return queries.astype(jnp.bfloat16)


def draw_response_lengths(key, part):
    key = jax.random.fold_in(key, 5)
    first, second, third = jax.random.split(key, 3)
    order = jax.random.permutation(first, SLOTS)
    full_slot = jax.random.randint(second, (), 0, SLOTS)
    slot = jnp.arange(SLOTS)
    chosen = slot == full_slot
    score = jnp.where(chosen, -1, order)
    rank = jnp.argsort(jnp.argsort(score, stable=True), stable=True)
    live = rank < RESP
    drawn = jax.random.randint(third, (SLOTS,), RLEN // 2, RLEN + 1)
    drawn = jnp.where(chosen, RLEN, drawn)
    return jnp.where(live, drawn, 0).astype(jnp.int32)


def shard_levels(key, shape, cuts, low, top_value):
    factor_of, own = 1.0, jax.random.fold_in(key, 6)
    for axis_at, parts in cuts:
        steps = jnp.exp(jax.random.uniform(jax.random.fold_in(own, axis_at), (parts,), jnp.float32, low / len(cuts), top_value / len(cuts)))
        factor_of = factor_of * jnp.repeat(steps, shape[axis_at] // parts).reshape([-1 if axis == axis_at else 1 for axis in range(len(shape))])
    return factor_of


def centred(own_key, extent, scale, reach, pieces=(), kind=jnp.bfloat16):
    array = jax.random.normal(own_key, extent, jnp.float32) * scale
    if len(pieces) > 0:
        array = shard_levels(own_key, extent, pieces, -0.22, 0.18) * array
    return jnp.clip(array, min=-reach, max=reach).astype(kind)


def setup_inputs(seed: int = 0) -> dict:
    arg_keys = jax.random.split(jax.random.key(seed), 8)
    return {
        "prompt_queries": draw_prompt_queries(jax.random.fold_in(arg_keys[7], 71), 0),
        "prompt_cache": draw_prompt_cache(jax.random.fold_in(arg_keys[7], 71), 0),
        "response_queries": draw_response_queries(jax.random.fold_in(arg_keys[7], 71), 0),
        "response_cache": centred(arg_keys[3], (RROWS, 2 * HD), 1.0, 6.0, ((0, 32),)),
        "prompt_cotangent": centred(arg_keys[4], (PROMPT, QH * HD), 1.0, 6.0, ((0, 32), (1, 8))),
        "response_cotangent": centred(arg_keys[5], (RROWS, QH * HD), 1.0, 6.0, ((0, 32), (1, 8))),
        "response_lengths": draw_response_lengths(jax.random.fold_in(arg_keys[7], 71), 0),
    }


def head_pass(query, keys, values, cotangent, mask, live):
    scale = 1.0 / math.sqrt(query.shape[1])
    scores = jnp.dot(query, keys.T, preferred_element_type=jnp.float32) * scale
    scores = jnp.where(mask, scores, -1e+30)
    highest = lax.optimization_barrier(jnp.max(scores, axis=1, keepdims=True))
    raised = jnp.where(mask, jnp.exp(scores - highest), 0.0)
    totals = lax.optimization_barrier(jnp.sum(raised, axis=1, keepdims=True)) + jnp.where(live, 0.0, 1.0)[:, None]
    probs = raised / totals
    rounded = probs.astype(jnp.bfloat16)
    attended = jnp.dot(rounded, values, preferred_element_type=jnp.float32)
    slopes = jnp.dot(cotangent, values.T, preferred_element_type=jnp.float32)
    offset = lax.optimization_barrier(jnp.sum(cotangent.astype(jnp.float32) * attended, axis=1, keepdims=True))
    score_grad = (probs * (slopes - offset)).astype(jnp.bfloat16)
    query_grad = jnp.dot(score_grad, keys, preferred_element_type=jnp.float32) * scale
    key_grad = jnp.dot(score_grad.T, query, preferred_element_type=jnp.float32) * scale
    value_grad = jnp.dot(rounded.T, cotangent, preferred_element_type=jnp.float32)
    return (attended.astype(jnp.bfloat16), query_grad.astype(jnp.bfloat16), key_grad, value_grad)

def merge_heads(stacked):
    return jnp.transpose(stacked, (1, 0, 2)).reshape(stacked.shape[1], -1)

def group_pass(queries, keys, values, cotangent, mask, live):
    width = keys.shape[1]
    heads = queries.shape[1] // width

    def one_head(head):
        start = head * width
        query = lax.dynamic_slice_in_dim(queries, start, width, 1)
        upstream = lax.dynamic_slice_in_dim(cotangent, start, width, 1)
        return head_pass(query, keys, values, upstream, mask, live)
    attended, query_grad, key_grad, value_grad = lax.map(one_head, jnp.arange(heads, dtype=jnp.int32))
    return (merge_heads(attended), merge_heads(query_grad), lax.optimization_barrier(jnp.sum(key_grad, axis=0)), lax.optimization_barrier(jnp.sum(value_grad, axis=0)))

def slot_pass(queries, cache, cotangent, length, prompt_keys, prompt_values):
    width = prompt_keys.shape[1]
    span = queries.shape[0]
    count = prompt_keys.shape[0]
    position = jnp.arange(span, dtype=jnp.int32)
    live = position < length
    own = (position[None, :] <= position[:, None]) & live[:, None]
    mask = jnp.concatenate([jnp.broadcast_to(live[:, None], (span, count)), own], axis=1)
    keys = jnp.concatenate([prompt_keys, cache[:, :width]], axis=0)
    values = jnp.concatenate([prompt_values, cache[:, width:]], axis=0)
    attended, query_grad, key_grad, value_grad = group_pass(queries, keys, values, cotangent, mask, live)
    prompt_part = jnp.concatenate([key_grad[:count], value_grad[:count]], axis=1)
    own_part = jnp.concatenate([key_grad[count:], value_grad[count:]], axis=1)
    return (attended, query_grad, prompt_part, own_part)

def maybe_slot(queries, cache, cotangent, length, prompt_keys, prompt_values):
    width = prompt_keys.shape[1]
    count = prompt_keys.shape[0]
    span = queries.shape[0]

    def busy(unused):
        return slot_pass(queries, cache, cotangent, length, prompt_keys, prompt_values)

    def empty(unused):
        return (jnp.zeros_like(queries), jnp.zeros_like(queries), jnp.zeros((count, 2 * width), jnp.float32), jnp.zeros((span, 2 * width), jnp.float32))
    return lax.cond(length > 0, busy, empty, 0)

def reference(prompt_queries, prompt_cache, response_queries, response_cache, prompt_cotangent, response_cotangent, response_lengths):
    width = prompt_cache.shape[1] // 2
    prompt_keys = prompt_cache[:, :width]
    prompt_values = prompt_cache[:, width:]
    rows = jnp.arange(PROMPT, dtype=jnp.int32)
    mask = rows[None, :] <= rows[:, None]
    live = jnp.ones((PROMPT,), dtype=jnp.bool_)
    prompt_output, prompt_adjoint, key_grad, value_grad = group_pass(prompt_queries, prompt_keys, prompt_values, prompt_cotangent, mask, live)
    start_total = jnp.concatenate([key_grad, value_grad], axis=1)

    def slot_step(carry, item):
        queries, cache, cotangent, length = item
        attended, query_grad, prompt_part, own_part = maybe_slot(queries, cache, cotangent, length, prompt_keys, prompt_values)
        return (carry + prompt_part, (attended, query_grad, own_part))
    items = (response_queries.reshape(SLOTS, RLEN, -1), response_cache.reshape(SLOTS, RLEN, -1), response_cotangent.reshape(SLOTS, RLEN, -1), response_lengths)
    prompt_total, (attended, query_grad, own_part) = lax.scan(slot_step, start_total, items)
    response_output = attended.reshape(RROWS, -1)
    response_adjoint = query_grad.reshape(RROWS, -1)
    response_cachegrad = own_part.reshape(RROWS, -1).astype(jnp.bfloat16)
    prompt_cachegrad = prompt_total.astype(jnp.bfloat16)
    return (prompt_output, response_output, prompt_adjoint, response_adjoint, prompt_cachegrad, response_cachegrad)
```

```python
import functools, math
import jax, jax.numpy as jnp
from jax import lax
from jax.experimental import pallas as pl
from jax.experimental.pallas import tpu as pltpu
f32=jnp.float32; bf16=jnp.bfloat16
HDIM=128

def dot(a,b): return jnp.dot(a,b,preferred_element_type=f32)

def attend(q,g,kv_at,kvt_at,segs,s_scr,pb_scr,live,add_grad,chunk):
    rb=q.shape[0]
    c=math.log2(math.e)/math.sqrt(HDIM)
    qt=q.astype(f32).T.astype(bf16); gt=g.astype(f32).T.astype(bf16)
    def rows(i): return pl.ds(pl.multiple_of(i*chunk,chunk),chunk)
    m=jnp.full((8,rb),-1e30,f32)
    for (which,base,lo,hi,mask) in segs:
        def step(i,m):
            s=dot(kv_at(which,i)[:,:HDIM],qt)
            if mask is not None: s=jnp.where(mask(i),s,-1e30)
            s_scr[rows(base+i),:rb]=s
            return jnp.maximum(m,jnp.max(s.reshape(chunk//8,8,rb),axis=0))
        m=lax.fori_loop(lo,hi,step,m)
    m=jnp.max(m,axis=0,keepdims=True)
    l=jnp.zeros((8,rb),f32)
    for (which,base,lo,hi,mask) in segs:
        def step(i,l):
            e=jnp.exp2((s_scr[rows(base+i),:rb]-m)*c)
            s_scr[rows(base+i),:rb]=e
            return l+jnp.sum(e.reshape(chunk//8,8,rb),axis=0)
        l=lax.fori_loop(lo,hi,step,l)
    inv=jnp.where(live,1.0/jnp.sum(l,axis=0,keepdims=True),0.0)
    ot=jnp.zeros((HDIM,rb),f32)
    for (which,base,lo,hi,mask) in segs:
        def step(i,ot):
            p=s_scr[rows(base+i),:rb]*inv
            pb=p.astype(bf16)
            pb_scr[rows(base+i),:rb]=pb
            return ot+dot(kvt_at(which,i)[HDIM:],pb)
        ot=lax.fori_loop(lo,hi,step,ot)
    delta=jnp.sum(gt.astype(f32)*ot,axis=0,keepdims=True)
    dqt=jnp.zeros((HDIM,rb),f32)
    for (which,base,lo,hi,mask) in segs:
        def step(i,dqt):
            dp=dot(kv_at(which,i)[:,HDIM:],gt)
            p=s_scr[rows(base+i),:rb]*inv
            ds=(p*(dp-delta)).astype(bf16)
            dv=dot(pb_scr[rows(base+i),:rb],g)
            dk=dot(ds,q)
            add_grad(which,i,dk,dv)
            return dqt+dot(kvt_at(which,i)[:HDIM],ds)
        dqt=lax.fori_loop(lo,hi,step,dqt)
    return ot.T.astype(bf16),(dqt*(1.0/math.sqrt(HDIM))).T.astype(bf16)

def kernel(RB,KC,info,qp,gp,kvp,qr,gr,kvr,op,dqp,our,dqr,dkv,dkvr,s_scr,pb_scr,kvt):
    length=info[0]; sidx=info[1]
    share=qp.shape[0]; count=kvp.shape[0]; span=qr.shape[0]
    nch=count//KC; nown=span//KC
    def rows(i): return pl.ds(pl.multiple_of(i*KC,KC),KC)
    def kv_at(which,i): return (kvp if which==0 else kvr)[rows(i),:]
    def kvt_at(which,i):
        return kvt[:,pl.ds(pl.multiple_of((i+(0 if which==0 else nch))*KC,KC),KC)]
    def tr(i,_):
        kvt[:,rows(i)]=kvp[rows(i),:].astype(f32).T.astype(bf16)
        return 0
    lax.fori_loop(0,nch,tr,0)
    zero=jnp.zeros((KC,2*HDIM),f32)
    def add(which,i,dk,dv):
        ref=dkv if which==0 else dkvr
        ref[rows(i),:HDIM]+=dk
        ref[rows(i),HDIM:]+=dv
    def put(which,i,dk,dv):
        ref=dkv if which==0 else dkvr
        ref[rows(i),:HDIM]=dk
        ref[rows(i),HDIM:]=dv
    def clear(i,_):
        dkv[rows(i),:]=zero
        return 0
    n=((sidx+1)*share+KC-1)//KC
    kio=lax.broadcasted_iota(jnp.int32,(KC,share),0)
    rio=lax.broadcasted_iota(jnp.int32,(KC,share),1)
    pmask=lambda i: i*KC+kio<=sidx*share+rio
    o,dq=attend(qp[...],gp[...],kv_at,kvt_at,[(0,0,0,n,pmask)],s_scr,pb_scr,True,put,KC)
    op[...]=o; dqp[...]=dq
    lax.fori_loop(n,nch,clear,0)
    @pl.when(length>0)
    def _():
        def tr2(i,_):
            kvt[:,pl.ds(pl.multiple_of((nch+i)*KC,KC),KC)]=kvr[rows(i),:].astype(f32).T.astype(bf16)
            dkvr[rows(i),:]=zero
            return 0
        lax.fori_loop(0,nown,tr2,0)
        for b in range(span//RB):
            ko=lax.broadcasted_iota(jnp.int32,(KC,RB),0)
            ro=lax.broadcasted_iota(jnp.int32,(KC,RB),1)
            omask=lambda i,b=b: i*KC+ko<=b*RB+ro
            live=b*RB+lax.broadcasted_iota(jnp.int32,(1,RB),1)<length
            full=(b*RB)//KC
            end=((b+1)*RB)//KC
            segs=[(0,0,0,nch,None)]
            if full>0: segs.append((1,nch,0,full,None))
            segs.append((1,nch,full,end,omask))
            o,dq=attend(qr[b*RB:(b+1)*RB,:],gr[b*RB:(b+1)*RB,:],kv_at,kvt_at,segs,s_scr,pb_scr,live,add,KC)
            our[b*RB:(b+1)*RB,:]=o
            dqr[b*RB:(b+1)*RB,:]=dq
    @pl.when(length==0)
    def _():
        our[...]=jnp.zeros_like(our); dqr[...]=jnp.zeros_like(dqr)
        dkvr[...]=jnp.zeros_like(dkvr)

def run(info,qp,gp,kvp,qr,gr,kvr,RB=512,KC=512):
    span=qr.shape[0]; count=kvp.shape[0]
    V=pl.BlockSpec(memory_space=pltpu.VMEM)
    return pl.pallas_call(
        functools.partial(kernel,RB,KC),
        out_shape=(jax.ShapeDtypeStruct(qp.shape,bf16),jax.ShapeDtypeStruct(qp.shape,bf16),
                   jax.ShapeDtypeStruct(qr.shape,bf16),jax.ShapeDtypeStruct(qr.shape,bf16),
                   jax.ShapeDtypeStruct(kvp.shape,f32),jax.ShapeDtypeStruct(kvr.shape,f32)),
        in_specs=[pl.BlockSpec(memory_space=pltpu.SMEM)]+[V]*6,
        out_specs=(V,)*6,
        scratch_shapes=[pltpu.VMEM((count+span,RB),f32),pltpu.VMEM((count+span,RB),bf16),pltpu.VMEM((2*HDIM,count+span),bf16)],
        compiler_params=pltpu.CompilerParams(vmem_limit_bytes=60*1024*1024),
        name="attention",
    )(info,qp,gp,kvp,qr,gr,kvr)


CORES = 2


def swap_cores(x, seq):
    return lax.ppermute(x, "seq", [(i, i ^ 1) for i in range(seq)])


def spread(x, axis, groups=None):
    return lax.all_to_all(x, axis, 0, 0, tiled=True, axis_index_groups=groups)


def on_device(qp, kvp, qr, kvr, gp, gr, lengths):
    seq = lax.axis_size("seq")
    heads = lax.axis_size("head")
    me = lax.axis_index("seq")
    head = lax.axis_index("head")
    core = me % CORES
    chips = seq // CORES
    columns = [[i * CORES + c for i in range(chips)] for c in range(CORES)]
    share, wide = kvp.shape

    other = swap_cores(kvp, seq)
    both = jnp.where(core == 0, jnp.concatenate([kvp, other]), jnp.concatenate([other, kvp]))
    part = CORES * share // (CORES * heads)
    piece = lax.dynamic_slice_in_dim(both, (core * heads + head) * part, part, 0)
    piece = spread(jnp.broadcast_to(piece[None], (chips, part, wide)), "seq", columns)
    half = spread(jnp.broadcast_to(piece[None], (heads, chips, part, wide)), "head")
    other = swap_cores(half, seq)
    whole = jnp.where(core == 0, jnp.stack([half, other]), jnp.stack([other, half]))
    whole = whole.reshape(CORES * heads, chips, part, wide).transpose(1, 0, 2, 3).reshape(-1, wide)

    info = jnp.stack([lengths[0], me.astype(jnp.int32)])
    op, dqp, our, dqr, dkv, dkvr = run(info, qp, gp, whole, qr, gr, kvr)

    view = dkv.reshape(chips, CORES, share, wide)
    mine = lax.dynamic_index_in_dim(view, core, 1, False)
    give = lax.dynamic_index_in_dim(view, 1 - core, 1, False)
    chip = mine + swap_cores(give, seq)
    strip = share // heads
    chip = chip.reshape(chips, heads, strip, wide).transpose(1, 0, 2, 3).reshape(heads, -1, wide)
    own = dkvr.reshape(heads, -1, wide)
    summed = spread(jnp.concatenate([chip, own], axis=1), "head").sum(0)
    cut = chips * strip
    mixed = spread(summed[:cut].reshape(chips, strip, wide), "seq", columns).sum(0)
    scale = jnp.where(jnp.arange(wide) < wide // 2, 1.0 / math.sqrt(wide // 2), 1.0).astype(f32)
    done = (jnp.concatenate([mixed, summed[cut:]]) * scale).astype(bf16)
    done = spread(jnp.broadcast_to(done[None], (heads,) + done.shape), "head")
    return (op, our, dqp, dqr, done[:, :strip].reshape(share, wide), done[:, strip:].reshape(-1, wide))


def solution(mesh):
    P = jax.sharding.PartitionSpec
    rows, cache = P("seq", "head"), P("seq", None)
    return jax.shard_map(
        on_device,
        mesh=mesh,
        in_specs=(rows, cache, rows, cache, rows, rows, P("seq")),
        out_specs=(rows, rows, rows, rows, cache, cache),
        check_vma=False,
    )
```

```python
import functools, math
import jax, jax.numpy as jnp
from jax import lax
from jax.experimental import pallas as pl
from jax.experimental.pallas import tpu as pltpu
f32=jnp.float32; bf16=jnp.bfloat16
D=128
RATE=math.log2(math.e)/math.sqrt(D)
FAR=1e30
OWN=256
SEQ=("x_hi","z","core")
HEAD=("y","x_lo")
PLANE=("x_hi","y","x_lo")
LONG=8
HEADS=8
CORE_CHIPS=16
ROWS=16

def dot(a,b): return jnp.dot(a,b,preferred_element_type=f32)
def flip(x): return x.astype(f32).T.astype(bf16)
def fold(x): return x.reshape(x.shape[0]//8,8,x.shape[1])
def rows(i,n): return pl.ds(i*n,n)
def loop(n,step,init):
    for i in range(n): init=step(i,init)
    return init

def key_place(core,start,n,share,strip):
    r=start+lax.broadcasted_iota(jnp.int32,(n,share),0)
    wide=lambda size: size.bit_length()-1
    x=r>>wide(strip*CORE_CHIPS//2); head=(r>>wide(strip))&(HEADS-1); z=(r>>wide(ROWS))&(LONG-1); t=r&(ROWS-1)
    return ((x*LONG+z)*2+core)*share+head*ROWS+t

def forward(KC,info,qp,gp,near,far,qr,gr,kvr,op,our,stat,dqo,dkvr,s,own):
    length=info[0]; first=info[1]*qp.shape[0]
    half=near.shape[0]; count=2*half; span=qr.shape[0]; share=qp.shape[0]; n=span+share
    qt=jnp.concatenate([flip(qr[...]),flip(qp[...])],axis=1)
    gt=jnp.concatenate([flip(gr[...]),flip(gp[...])],axis=1)
    def part(i):
        return (near if i*KC<half else far)[pl.ds(i*KC%half,KC),:]
    def seen(i):
        place=key_place(info[2] if i*KC<half else 1-info[2],i*KC%half,KC,share,half//CORE_CHIPS)
        return place<=first+lax.broadcasted_iota(jnp.int32,(KC,share),1)
    tri=lax.broadcasted_iota(jnp.int32,(OWN,OWN),0)<=lax.broadcasted_iota(jnp.int32,(OWN,OWN),1)
    def top(i,m):
        x=dot(part(i)[:,:D],qt)
        x=jnp.concatenate([x[:,:span],jnp.where(seen(i),x[:,span:],-FAR)],axis=1)
        s[rows(i,KC),:]=x
        return jnp.maximum(m,jnp.max(fold(x),axis=0))
    m=loop(count//KC,top,jnp.full((8,n),-FAR,f32))
    mr=m[:,:span]
    for j in range(span//OWN):
        x=dot(kvr[j*OWN:(j+1)*OWN,:D],qt[:,j*OWN:span])
        d=jnp.where(tri,x[:,:OWN],-FAR)
        x=d if x.shape[1]==OWN else jnp.concatenate([d,x[:,OWN:]],axis=1)
        own[j*OWN:(j+1)*OWN,j*OWN:span]=x
        y=jnp.max(fold(x),axis=0)
        y=jnp.maximum(mr[:,j*OWN:],y)
        mr=y if j==0 else jnp.concatenate([mr[:,:j*OWN],y],axis=1)
    m=jnp.max(jnp.concatenate([mr,m[:,span:]],axis=1),axis=0,keepdims=True)*RATE
    def total(i,l):
        return l+jnp.sum(fold(jnp.exp2(s[rows(i,KC),:]*RATE-m)),axis=0)
    l=loop(count//KC,total,jnp.zeros((8,n),f32))
    lr=l[:,:span]
    for j in range(span//OWN):
        y=lr[:,j*OWN:]+jnp.sum(fold(jnp.exp2(own[j*OWN:(j+1)*OWN,j*OWN:span]*RATE-m[:,j*OWN:span])),axis=0)
        lr=y if j==0 else jnp.concatenate([lr[:,:j*OWN],y],axis=1)
    l=jnp.sum(jnp.concatenate([lr,l[:,span:]],axis=1),axis=0,keepdims=True)
    level=m+jnp.log2(l)
    at=lax.broadcasted_iota(jnp.int32,(1,n),1)
    level=jnp.where((at<length)|(at>=span),level,FAR)
    def attend(i,o):
        p=jnp.exp2(s[rows(i,KC),:]*RATE-level).astype(bf16)
        return o+dot(flip(part(i)[:,D:]),p)
    o=loop(count//KC,attend,jnp.zeros((D,n),f32))
    tail=o[:,span:]
    o=o[:,:span]
    for j in range(span//OWN):
        p=jnp.exp2(own[j*OWN:(j+1)*OWN,j*OWN:span]*RATE-level[:,j*OWN:span]).astype(bf16)
        y=o[:,j*OWN:]+dot(flip(kvr[j*OWN:(j+1)*OWN,D:]),p)
        o=y if j==0 else jnp.concatenate([o[:,:j*OWN],y],axis=1)
    our[...]=o.T.astype(bf16)
    op[...]=tail.T.astype(bf16)
    delta=jnp.sum(gt.astype(f32)*jnp.concatenate([o,tail],axis=1),axis=0,keepdims=True)
    stat[...]=jnp.concatenate([jnp.broadcast_to(level,(8,n)),jnp.broadcast_to(delta,(8,n))],axis=0)
    dq=jnp.zeros((D,span),f32)
    for j in range(span//OWN):
        a=slice(j*OWN,(j+1)*OWN); b=slice(j*OWN,span)
        p=jnp.exp2(own[a,b]*RATE-level[:,b])
        dp=dot(kvr[a,D:],gt[:,b])
        ds=(p*(dp-delta[:,b])).astype(bf16)
        dkvr[a,D:]=dot(p.astype(bf16),gr[b,:])
        dkvr[a,:D]=dot(ds,qr[b,:])
        y=dq[:,b]+dot(flip(kvr[a,:D]),ds)
        dq=y if j==0 else jnp.concatenate([dq[:,:j*OWN],y],axis=1)
    dqo[...]=dq

def backward(KC,info,qp,gp,near,far,qr,gr,stat,dqo,dqp,dqr,dnear,dfar):
    first=info[1]*qp.shape[0]
    half=near.shape[0]; count=2*half; span=qr.shape[0]; share=qp.shape[0]; n=span+share
    qt=jnp.concatenate([flip(qr[...]),flip(qp[...])],axis=1)
    gt=jnp.concatenate([flip(gr[...]),flip(gp[...])],axis=1)
    q=jnp.concatenate([qr[...],qp[...]],axis=0)
    g=jnp.concatenate([gr[...],gp[...]],axis=0)
    level=stat[:1,:]; delta=stat[8:9,:]
    def part(i):
        return (near if i*KC<half else far)[pl.ds(i*KC%half,KC),:]
    def seen(i):
        place=key_place(info[2] if i*KC<half else 1-info[2],i*KC%half,KC,share,half//CORE_CHIPS)
        return place<=first+lax.broadcasted_iota(jnp.int32,(KC,share),1)
    def step(i,dq):
        x=dot(part(i)[:,:D],qt)
        dp=dot(part(i)[:,D:],gt)
        p=jnp.exp2(x*RATE-level)
        grad=dnear if i*KC<half else dfar
        a=pl.ds(i*KC%half,KC)
        p=jnp.concatenate([p[:,:span],jnp.where(seen(i),p[:,span:],0.0)],axis=1)
        ds=(p*(dp-delta)).astype(bf16)
        grad[a,D:]=dot(p.astype(bf16),g)
        grad[a,:D]=dot(ds,q)
        return dq+dot(flip(part(i)[:,:D]),ds)
    dq=loop(count//KC,step,jnp.concatenate([dqo[...],jnp.zeros((D,share),f32)],axis=1))
    dq=(dq*(1.0/math.sqrt(D))).T.astype(bf16)
    dqr[...]=dq[:span]; dqp[...]=dq[span:]

V=pl.BlockSpec(memory_space=pltpu.VMEM)
SM=pl.BlockSpec(memory_space=pltpu.SMEM)
def shape(s,t=f32): return jax.ShapeDtypeStruct(s,t)

def run_forward(info,qp,gp,near,far,qr,gr,kvr,KC=512):
    span=qr.shape[0]; half=near.shape[0]; share=qp.shape[0]; n=span+share
    return pl.pallas_call(functools.partial(forward,KC),
        out_shape=(shape(qp.shape,bf16),shape(qr.shape,bf16),shape((16,n)),shape((D,span)),shape(kvr.shape)),
        in_specs=[SM]+[V]*7,out_specs=(V,)*5,
        scratch_shapes=[pltpu.VMEM((2*half,n),f32),pltpu.VMEM((span,span),f32)],
        cost_estimate=pl.CostEstimate(flops=5*n*half*2*D,bytes_accessed=2**23,transcendentals=4*n*half),
        compiler_params=pltpu.CompilerParams(vmem_limit_bytes=56*1024*1024),name="forward")(info,qp,gp,near,far,qr,gr,kvr)

def run_backward(info,qp,gp,near,far,qr,gr,stat,dqo,KC=512):
    n=stat.shape[1]; half=near.shape[0]
    return pl.pallas_call(functools.partial(backward,KC),
        out_shape=(shape(qp.shape,bf16),shape(qr.shape,bf16),shape(near.shape),shape(far.shape)),
        in_specs=[SM]+[V]*8,out_specs=(V,)*4,
        cost_estimate=pl.CostEstimate(flops=10*n*half*2*D,bytes_accessed=2**23,transcendentals=2*n*half),
        compiler_params=pltpu.CompilerParams(vmem_limit_bytes=56*1024*1024),name="backward")(info,qp,gp,near,far,qr,gr,stat,dqo)

def swap(x): return lax.ppermute(x,"core",[(0,1),(1,0)])
def spread(x,axes): return lax.all_to_all(x,axes,0,0,tiled=True)
def copies(x,n): return jnp.broadcast_to(x[None],(n,)+x.shape)

def on_device(qp,kvp,qr,kvr,gp,gr,lengths):
    core=lax.axis_index("core")
    head=lax.axis_index(HEAD)
    info=jnp.stack([lengths[0],lax.axis_index(SEQ).astype(jnp.int32),core.astype(jnp.int32)])
    piece=lax.dynamic_slice_in_dim(kvp,head*ROWS,ROWS,0)
    line=spread(copies(piece,LONG),"z")
    near=spread(copies(line,CORE_CHIPS),PLANE).reshape(-1,2*D)
    far=swap(near)
    op,our,stat,dqo,own=run_forward(info,qp,gp,near,far,qr,gr,kvr)
    own=spread(own.reshape(HEADS,-1,2*D),HEAD).sum(0)
    dqp,dqr,dnear,dfar=run_backward(info,qp,gp,near,far,qr,gr,stat,dqo)
    chip=dnear+swap(dfar)
    line=spread(chip.reshape(CORE_CHIPS,-1,2*D),PLANE).sum(0)
    strip=spread(line.reshape(LONG,ROWS,2*D),"z").sum(0)
    scale=jnp.where(jnp.arange(2*D)<D,1.0/math.sqrt(D),1.0).astype(f32)
    done=(jnp.concatenate([strip,own])*scale).astype(bf16)
    done=spread(copies(done,HEADS),HEAD)
    return (op,our,dqp,dqr,done[:,:ROWS].reshape(-1,2*D),done[:,ROWS:].reshape(-1,2*D))

def solution(mesh):
    P=jax.sharding.PartitionSpec
    fine=jax.sharding.Mesh(mesh.devices.reshape(2,LONG,2,4,2),SEQ+HEAD)
    rows_,cache=P(SEQ,HEAD),P(SEQ,None)
    return jax.shard_map(on_device,mesh=fine,
        in_specs=(rows_,cache,rows_,cache,rows_,rows_,P(SEQ)),
        out_specs=(rows_,rows_,rows_,rows_,cache,cache),check_vma=False)
```

```python
import functools, math
import jax, jax.numpy as jnp
from jax import lax
from jax.experimental import pallas as pl
from jax.experimental.pallas import tpu as pltpu
f32=jnp.float32; bf16=jnp.bfloat16
D=128
RATE=math.log2(math.e)/math.sqrt(D)
FAR=1e30
OWN=256
SEQ=("x_hi","z","core")
HEAD=("y","x_lo")
PLANE=("x_hi","y","x_lo")
LONG=8
HEADS=8
TILE=16
CORE_CHIPS=16
ROWS=16

def dot(a,b): return jnp.dot(a,b,preferred_element_type=f32)
def flip(x): return x.astype(f32).T.astype(bf16)
def fold(x): return x.reshape(x.shape[0]//8,8,x.shape[1])
def rows(i,n): return pl.ds(i*n,n)
def loop(n,step,init):
    for i in range(n): init=step(i,init)
    return init

def key_place(core,start,n,share,strip):
    r=start+lax.broadcasted_iota(jnp.int32,(n,share),0)
    wide=lambda size: size.bit_length()-1
    x=r>>wide(strip*CORE_CHIPS//2); head=(r>>wide(strip))&(HEADS-1); z=(r>>wide(ROWS))&(LONG-1); t=r&(ROWS-1)
    return ((x*LONG+z)*2+core)*share+head*ROWS+t

def seq_place():
    return (lax.axis_index(SEQ[0])*LONG+lax.axis_index(SEQ[1]))*2+lax.axis_index(SEQ[2])

def forward(KC,info,qp,gp,near,far,qr,gr,kvr,op,our,stat,dqo,own2,s,own):
    length=info[0]; first=seq_place()*qp.shape[0]
    core=lax.axis_index("core")
    half=near.shape[0]; count=2*half; span=qr.shape[0]; share=qp.shape[0]; n=span+share
    qt=jnp.concatenate([flip(qr[...]),flip(qp[...])],axis=1)
    gt=jnp.concatenate([flip(gr[...]),flip(gp[...])],axis=1)
    def part(i):
        return (near if i*KC<half else far)[pl.ds(i*KC%half,KC),:]
    def seen(i):
        place=key_place(core if i*KC<half else 1-core,i*KC%half,KC,share,half//CORE_CHIPS)
        return place<=first+lax.broadcasted_iota(jnp.int32,(KC,share),1)
    tri=lax.broadcasted_iota(jnp.int32,(OWN,OWN),0)<=lax.broadcasted_iota(jnp.int32,(OWN,OWN),1)
    def top(i,m):
        x=dot(part(i)[:,:D],qt)
        x=jnp.concatenate([x[:,:span],jnp.where(seen(i),x[:,span:],-FAR)],axis=1)
        s[rows(i,KC),:]=x
        return jnp.maximum(m,jnp.max(fold(x),axis=0))
    m=loop(count//KC,top,jnp.full((8,n),-FAR,f32))
    mr=m[:,:span]
    for j in range(span//OWN):
        x=dot(kvr[j*OWN:(j+1)*OWN,:D],qt[:,j*OWN:span])
        d=jnp.where(tri,x[:,:OWN],-FAR)
        x=d if x.shape[1]==OWN else jnp.concatenate([d,x[:,OWN:]],axis=1)
        own[j*OWN:(j+1)*OWN,j*OWN:span]=x
        y=jnp.max(fold(x),axis=0)
        y=jnp.maximum(mr[:,j*OWN:],y)
        mr=y if j==0 else jnp.concatenate([mr[:,:j*OWN],y],axis=1)
    m=jnp.max(jnp.concatenate([mr,m[:,span:]],axis=1),axis=0,keepdims=True)*RATE
    def total(i,l):
        return l+jnp.sum(fold(jnp.exp2(s[rows(i,KC),:]*RATE-m)),axis=0)
    l=loop(count//KC,total,jnp.zeros((8,n),f32))
    lr=l[:,:span]
    for j in range(span//OWN):
        y=lr[:,j*OWN:]+jnp.sum(fold(jnp.exp2(own[j*OWN:(j+1)*OWN,j*OWN:span]*RATE-m[:,j*OWN:span])),axis=0)
        lr=y if j==0 else jnp.concatenate([lr[:,:j*OWN],y],axis=1)
    l=jnp.sum(jnp.concatenate([lr,l[:,span:]],axis=1),axis=0,keepdims=True)
    level=m+jnp.log2(l)
    at=lax.broadcasted_iota(jnp.int32,(1,n),1)
    level=jnp.where((at<length)|(at>=span),level,FAR)
    def attend(i,o):
        p=jnp.exp2(s[rows(i,KC),:]*RATE-level).astype(bf16)
        return o+dot(flip(part(i)[:,D:]),p)
    o=loop(count//KC,attend,jnp.zeros((D,n),f32))
    tail=o[:,span:]
    o=o[:,:span]
    for j in range(span//OWN):
        p=jnp.exp2(own[j*OWN:(j+1)*OWN,j*OWN:span]*RATE-level[:,j*OWN:span]).astype(bf16)
        y=o[:,j*OWN:]+dot(flip(kvr[j*OWN:(j+1)*OWN,D:]),p)
        o=y if j==0 else jnp.concatenate([o[:,:j*OWN],y],axis=1)
    our[...]=o.T.astype(bf16)
    op[...]=tail.T.astype(bf16)
    delta=jnp.sum(gt.astype(f32)*jnp.concatenate([o,tail],axis=1),axis=0,keepdims=True)
    stat[...]=jnp.concatenate([jnp.broadcast_to(level,(8,n)),jnp.broadcast_to(delta,(8,n))],axis=0)
    dq=jnp.zeros((D,span),f32)
    for j in range(span//OWN):
        a=slice(j*OWN,(j+1)*OWN); b=slice(j*OWN,span)
        p=jnp.exp2(own[a,b]*RATE-level[:,b])
        dp=dot(kvr[a,D:],gt[:,b])
        ds=(p*(dp-delta[:,b])).astype(bf16)
        dv=dot(p.astype(bf16),gr[b,:])
        dk=dot(ds,qr[b,:])
        strip=span//HEADS
        for t in range(OWN//strip):
            u=slice(t*strip,(t+1)*strip)
            own2[j*(OWN//strip)+t,:,D:]=dv[u]
            own2[j*(OWN//strip)+t,:,:D]=dk[u]
        y=dq[:,b]+dot(flip(kvr[a,:D]),ds)
        dq=y if j==0 else jnp.concatenate([dq[:,:j*OWN],y],axis=1)
    dqo[...]=jnp.concatenate([dq,jnp.zeros((D,share),f32)],axis=1)

def backward(KC,last,qp,gp,kv,qr,gr,stat,dqo,dq_out,grad):
    first=seq_place()*qp.shape[0]
    core=lax.axis_index("core")
    if not last: core=1-core
    half=kv.shape[0]; span=qr.shape[0]; share=qp.shape[0]
    qt=jnp.concatenate([flip(qr[...]),flip(qp[...])],axis=1)
    gt=jnp.concatenate([flip(gr[...]),flip(gp[...])],axis=1)
    q=jnp.concatenate([qr[...],qp[...]],axis=0)
    g=jnp.concatenate([gr[...],gp[...]],axis=0)
    level=stat[:1,:]; delta=stat[8:9,:]
    def seen(i):
        place=key_place(core,i*KC,KC,share,half//CORE_CHIPS)
        return place<=first+lax.broadcasted_iota(jnp.int32,(KC,share),1)
    def step(i,dq):
        a=rows(i,KC)
        x=dot(kv[a,:D],qt)
        dp=dot(kv[a,D:],gt)
        p=jnp.exp2(x*RATE-level)
        p=jnp.concatenate([p[:,:span],jnp.where(seen(i),p[:,span:],0.0)],axis=1)
        ds=(p*(dp-delta)).astype(bf16)
        grad[a,D:]=dot(p.astype(bf16),g)
        grad[a,:D]=dot(ds,q)
        return dq+dot(flip(kv[a,:D]),ds)
    dq=loop(half//KC,step,dqo[...])
    if not last: dq_out[...]=dq
    else: dq_out[...]=(dq*(1.0/math.sqrt(D))).T.astype(bf16)

V=pl.BlockSpec(memory_space=pltpu.VMEM)
SM=pl.BlockSpec(memory_space=pltpu.SMEM)
def shape(s,t=f32): return jax.ShapeDtypeStruct(s,t)

def run_forward(lengths,qp,gp,near,far,qr,gr,kvr,KC=512):
    span=qr.shape[0]; half=near.shape[0]; share=qp.shape[0]; n=span+share
    return pl.pallas_call(functools.partial(forward,KC),
        out_shape=(shape(qp.shape,bf16),shape(qr.shape,bf16),shape((16,n)),shape((D,n)),shape((HEADS,span//HEADS,2*D))),
        in_specs=[SM]+[V]*7,out_specs=(V,)*5,
        scratch_shapes=[pltpu.VMEM((2*half,n),f32),pltpu.VMEM((span,span),f32)],
        cost_estimate=pl.CostEstimate(flops=5*n*half*2*D,bytes_accessed=2**23,transcendentals=4*n*half),
        compiler_params=pltpu.CompilerParams(vmem_limit_bytes=46*1024*1024),name="forward")(lengths,qp,gp,near,far,qr,gr,kvr)

def run_backward(last,qp,gp,kv,qr,gr,stat,dqo,KC=512):
    n=stat.shape[1]; half=kv.shape[0]
    return pl.pallas_call(functools.partial(backward,KC,last),
        out_shape=(shape((n,D),bf16) if last else shape((D,n)),shape(kv.shape)),
        in_specs=[V]*7,out_specs=(V,)*2,
        cost_estimate=pl.CostEstimate(flops=50*n*half*2*D,bytes_accessed=2**22,transcendentals=n*half),
        compiler_params=pltpu.CompilerParams(vmem_limit_bytes=28*1024*1024),name="backward")(qp,gp,kv,qr,gr,stat,dqo)

def swap(x): return lax.ppermute(x,"core",[(0,1),(1,0)])
def spread(x,axes): return lax.all_to_all(x,axes,0,0,tiled=True)
def copies(x,n): return jnp.broadcast_to(x[None],(n,)+x.shape)

def pack(x):
    top=jnp.maximum(jnp.max(jnp.abs(x),axis=1,keepdims=True),2.0**-100)
    power=jnp.ceil(jnp.log2(top))
    rest=jnp.broadcast_to(power,(x.shape[0],TILE,x.shape[2]))
    return jnp.concatenate([x*jnp.exp2(-power),rest],axis=1).astype(jnp.float16)

def unpack_sum(x):
    power=x[:,-1:].astype(f32)
    return jnp.sum(x[:,:-TILE].astype(f32)*jnp.exp2(power),axis=0)

def on_device(qp,kvp,qr,kvr,gp,gr,lengths):
    head=lax.axis_index(HEAD)
    span=qr.shape[0]
    piece=lax.dynamic_slice_in_dim(kvp,head*ROWS,ROWS,0)
    line=spread(copies(piece,LONG),"z")
    near=spread(copies(line,CORE_CHIPS),PLANE).reshape(-1,2*D)
    far=swap(near)
    op,our,stat,dq,own=run_forward(lengths,qp,gp,near,far,qr,gr,kvr)
    own=spread(pack(own),HEAD)
    dq,dfar=run_backward(False,qp,gp,far,qr,gr,stat,dq)
    chip=swap(dfar)
    dq,dnear=run_backward(True,qp,gp,near,qr,gr,stat,dq)
    chip,own=lax.optimization_barrier((chip,own))
    own=unpack_sum(own)
    chip=chip+dnear
    line=unpack_sum(spread(pack(chip.reshape(CORE_CHIPS,-1,2*D)),PLANE))
    strip=spread(line.reshape(LONG,ROWS,2*D),"z").sum(0)
    scale=jnp.where(jnp.arange(2*D)<D,1.0/math.sqrt(D),1.0).astype(f32)
    done=(jnp.concatenate([strip,own])*scale).astype(bf16)
    done=spread(copies(done,HEADS),HEAD)
    return (op,our,dq[span:],dq[:span],done[:,:ROWS].reshape(-1,2*D),done[:,ROWS:].reshape(-1,2*D))

def solution(mesh):
    P=jax.sharding.PartitionSpec
    fine=jax.sharding.Mesh(mesh.devices.reshape(2,LONG,2,4,2),SEQ+HEAD)
    rows_,cache=P(SEQ,HEAD),P(SEQ,None)
    return jax.shard_map(on_device,mesh=fine,
        in_specs=(rows_,cache,rows_,cache,rows_,rows_,P(SEQ)),
        out_specs=(rows_,rows_,rows_,rows_,cache,cache),check_vma=False)
```

```python
import functools, math
import jax, jax.numpy as jnp
from jax import lax
from jax.experimental import pallas as pl
from jax.experimental.pallas import tpu as pltpu
f32=jnp.float32; bf16=jnp.bfloat16
D=128
SCALE=1.0/math.sqrt(D)
RATE=math.log2(math.e)*SCALE
FAR=1e30
OWN=256
SEQ=("x_hi","z","core")
HEAD=("y","x_lo")
PLANE=("x_hi","y","x_lo")
LONG=8
HEADS=8
LINES=4
TILE=8
CORE_CHIPS=16
ROWS=16

def dot(a,b): return jnp.dot(a,b,preferred_element_type=f32)
def flip(x): return x.astype(f32).T.astype(bf16)
def fold(x): return x.reshape(x.shape[0]//8,8,x.shape[1])
def rows(i,n): return pl.ds(i*n,n)
def loop(n,step,init):
    for i in range(n): init=step(i,init)
    return init

def key_place(core,start,n,share,strip):
    r=start+lax.broadcasted_iota(jnp.int32,(n,share),0)
    wide=lambda size: size.bit_length()-1
    x=r>>wide(strip*CORE_CHIPS//2); head=(r>>wide(strip))&(HEADS-1); z=(r>>wide(ROWS))&(LONG-1); t=r&(ROWS-1)
    return ((x*LONG+z)*2+core)*share+head*ROWS+t

def pack(ref,b,cols,x):
    n=x.shape[0]
    power=jnp.ceil(jnp.log2(jnp.maximum(jnp.max(jnp.abs(x),axis=0,keepdims=True),2.0**-100)))
    ref[*b,:n,cols]=x*jnp.exp2(-power)
    ref[*b,n:,cols]=jnp.broadcast_to(power,(TILE,x.shape[1]))

KEYS,VALUES=slice(0,D),slice(D,2*D)

def seq_place():
    return (lax.axis_index(SEQ[0])*LONG+lax.axis_index(SEQ[1]))*2+lax.axis_index(SEQ[2])

def forward(KC,info,qp,gp,near,far,qr,gr,kvr,op,our,carry,own2,s,own):
    length=info[0]; first=seq_place()*qp.shape[0]
    core=lax.axis_index("core")
    half=near.shape[0]; count=2*half; span=qr.shape[0]; share=qp.shape[0]; n=span+share
    qt=jnp.concatenate([flip(qr[...]),flip(qp[...])],axis=1)
    gt=jnp.concatenate([flip(gr[...]),flip(gp[...])],axis=1)
    def part(i):
        return (near if i*KC<half else far)[pl.ds(i*KC%half,KC),:]
    def seen(i):
        place=key_place(core if i*KC<half else 1-core,i*KC%half,KC,share,half//CORE_CHIPS)
        return place<=first+lax.broadcasted_iota(jnp.int32,(KC,share),1)
    tri=lax.broadcasted_iota(jnp.int32,(OWN,OWN),0)<=lax.broadcasted_iota(jnp.int32,(OWN,OWN),1)
    def top(i,m):
        x=dot(part(i)[:,:D],qt)
        x=jnp.concatenate([x[:,:span],jnp.where(seen(i),x[:,span:],-FAR)],axis=1)
        s[rows(i,KC),:]=x
        return jnp.maximum(m,jnp.max(fold(x),axis=0))
    m=loop(count//KC,top,jnp.full((8,n),-FAR,f32))
    mr=m[:,:span]
    for j in range(span//OWN):
        x=dot(kvr[j*OWN:(j+1)*OWN,:D],qt[:,j*OWN:span])
        d=jnp.where(tri,x[:,:OWN],-FAR)
        x=d if x.shape[1]==OWN else jnp.concatenate([d,x[:,OWN:]],axis=1)
        own[j*OWN:(j+1)*OWN,j*OWN:span]=x
        y=jnp.max(fold(x),axis=0)
        y=jnp.maximum(mr[:,j*OWN:],y)
        mr=y if j==0 else jnp.concatenate([mr[:,:j*OWN],y],axis=1)
    m=jnp.max(jnp.concatenate([mr,m[:,span:]],axis=1),axis=0,keepdims=True)*RATE
    def total(i,l):
        e=jnp.exp2(s[rows(i,KC),:]*RATE-m)
        s[rows(i,KC),:]=e
        return l+jnp.sum(fold(e),axis=0)
    l=loop(count//KC,total,jnp.zeros((8,n),f32))
    lr=l[:,:span]
    for j in range(span//OWN):
        y=lr[:,j*OWN:]+jnp.sum(fold(jnp.exp2(own[j*OWN:(j+1)*OWN,j*OWN:span]*RATE-m[:,j*OWN:span])),axis=0)
        lr=y if j==0 else jnp.concatenate([lr[:,:j*OWN],y],axis=1)
    l=jnp.sum(jnp.concatenate([lr,l[:,span:]],axis=1),axis=0,keepdims=True)
    level=m+jnp.log2(l)
    at=lax.broadcasted_iota(jnp.int32,(1,n),1)
    live=(at<length)|(at>=span)
    inv=jnp.where(live,1.0/l,0.0)
    level=jnp.where(live,level,FAR)
    def attend(i,o):
        p=(s[rows(i,KC),:]*inv).astype(bf16)
        return o+dot(flip(part(i)[:,D:]),p)
    o=loop(count//KC,attend,jnp.zeros((D,n),f32))
    tail=o[:,span:]
    o=o[:,:span]
    for j in range(span//OWN):
        p=jnp.exp2(own[j*OWN:(j+1)*OWN,j*OWN:span]*RATE-level[:,j*OWN:span]).astype(bf16)
        y=o[:,j*OWN:]+dot(flip(kvr[j*OWN:(j+1)*OWN,D:]),p)
        o=y if j==0 else jnp.concatenate([o[:,:j*OWN],y],axis=1)
    our[...]=o.T.astype(bf16)
    op[...]=tail.T.astype(bf16)
    delta=jnp.sum(gt.astype(f32)*jnp.concatenate([o,tail],axis=1),axis=0,keepdims=True)
    carry[D:D+8,:]=jnp.broadcast_to(level,(8,n))
    carry[D+8:,:]=jnp.broadcast_to(delta,(8,n))
    dq=jnp.zeros((D,span),f32)
    for j in range(span//OWN):
        a=slice(j*OWN,(j+1)*OWN); b=slice(j*OWN,span)
        p=jnp.exp2(own[a,b]*RATE-level[:,b])
        dp=dot(kvr[a,D:],gt[:,b])
        ds=(p*(dp-delta[:,b])).astype(bf16)
        dv=dot(p.astype(bf16),gr[b,:])
        dk=dot(ds,qr[b,:])*SCALE
        strip=span//HEADS
        for t in range(OWN//strip):
            u=slice(t*strip,(t+1)*strip)
            x,y=divmod(j*(OWN//strip)+t,LINES)
            at=(x^lax.axis_index("x_lo"),(y-lax.axis_index("y"))&(LINES-1))
            pack(own2,at,VALUES,dv[u])
            pack(own2,at,KEYS,dk[u])
        y=dq[:,b]+dot(flip(kvr[a,:D]),ds)
        dq=y if j==0 else jnp.concatenate([dq[:,:j*OWN],y],axis=1)
    carry[:D,:]=jnp.concatenate([dq,jnp.zeros((D,share),f32)],axis=1)

def half_block(kv): return kv.shape[0]//CORE_CHIPS

def backward(KC,last,qp,gp,kv,qr,gr,carry,*out):
    if last: other,*out=out
    *out,grad=out
    block=half_block(kv)
    first=seq_place()*qp.shape[0]
    core=lax.axis_index("core")
    if not last: core=1-core
    half=kv.shape[0]; span=qr.shape[0]; share=qp.shape[0]
    qt=jnp.concatenate([flip(qr[...]),flip(qp[...])],axis=1)
    gt=jnp.concatenate([flip(gr[...]),flip(gp[...])],axis=1)
    q=jnp.concatenate([qr[...],qp[...]],axis=0)
    g=jnp.concatenate([gr[...],gp[...]],axis=0)
    level=carry[D:D+1,:]; delta=carry[D+8:D+9,:]
    def seen(i):
        place=key_place(core,i*KC,KC,share,half//CORE_CHIPS)
        return place<=first+lax.broadcasted_iota(jnp.int32,(KC,share),1)
    def step(i,dq):
        a=rows(i,KC)
        x=dot(kv[a,:D],qt)
        dp=dot(kv[a,D:],gt)
        p=jnp.exp2(x*RATE-level)
        p=jnp.concatenate([p[:,:span],jnp.where(seen(i),p[:,span:],0.0)],axis=1)
        ds=(p*(dp-delta)).astype(bf16)
        dv=dot(p.astype(bf16),g)
        dk=dot(ds,q)*SCALE
        if last:
            dv=dv+other[a,D:]
            dk=dk+other[a,:D]
            for t in range(KC//block):
                u=slice(t*block,(t+1)*block)
                pack(grad,(i*(KC//block)+t,),VALUES,dv[u])
                pack(grad,(i*(KC//block)+t,),KEYS,dk[u])
        else:
            grad[a,D:]=dv
            grad[a,:D]=dk
        return dq+dot(flip(kv[a,:D]),ds)
    dq=loop(half//KC,step,carry[:D,:])
    if not last:
        out[0][:D,:]=dq
        out[0][D:,:]=carry[D:,:]
    else:
        dq=(dq*SCALE).T.astype(bf16)
        out[0][...]=dq[:span]
        out[1][...]=dq[span:]

V=pl.BlockSpec(memory_space=pltpu.VMEM)
SM=pl.BlockSpec(memory_space=pltpu.SMEM)
def shape(s,t=f32): return jax.ShapeDtypeStruct(s,t)

def run_forward(lengths,qp,gp,near,far,qr,gr,kvr,KC=512):
    span=qr.shape[0]; half=near.shape[0]; share=qp.shape[0]; n=span+share
    return pl.pallas_call(functools.partial(forward,KC),
        out_shape=(shape(qp.shape,bf16),shape(qr.shape,bf16),shape((D+16,n)),shape((2,LINES,span//HEADS+TILE,2*D))),
        in_specs=[SM]+[V]*7,out_specs=(V,)*4,
        scratch_shapes=[pltpu.VMEM((2*half,n),f32),pltpu.VMEM((span,span),f32)],
        cost_estimate=pl.CostEstimate(flops=5*n*half*2*D,bytes_accessed=2**23,transcendentals=4*n*half),
        compiler_params=pltpu.CompilerParams(vmem_limit_bytes=46*1024*1024),name="forward")(lengths,qp,gp,near,far,qr,gr,kvr)

def run_backward(last,qp,gp,kv,qr,gr,carry,*other,KC=512):
    n=carry.shape[1]; half=kv.shape[0]
    return pl.pallas_call(functools.partial(backward,KC,last),
        out_shape=((shape(qr.shape,bf16),shape(qp.shape,bf16)) if last else (shape(carry.shape),))+(shape((CORE_CHIPS,half_block(kv)+TILE,2*D)) if last else shape(kv.shape),),
        in_specs=[V]*(6+last),out_specs=(V,)*(2+last),
        cost_estimate=pl.CostEstimate(flops=50*n*half*2*D,bytes_accessed=2**22,transcendentals=n*half),
        compiler_params=pltpu.CompilerParams(vmem_limit_bytes=28*1024*1024),name="backward")(qp,gp,kv,qr,gr,carry,*other)

def swap(x): return lax.ppermute(x,"core",[(0,1),(1,0)])
def spread(x,axes): return lax.all_to_all(x,axes,0,0,tiled=True)
def copies(x,n): return jnp.broadcast_to(x[None],(n,)+x.shape)

def unpack(x):
    rest=jnp.exp2(x[:,-TILE:].astype(f32))
    x=x[:,:-TILE].astype(f32).reshape(x.shape[0],-1,TILE,x.shape[2])
    return x*rest[:,None]

def turn(x,by): return lax.ppermute(x,"y",[(i,(i+by)%LINES) for i in range(LINES)])

def on_device(qp,kvp,qr,kvr,gp,gr,lengths):
    head=lax.axis_index(HEAD)
    piece=lax.dynamic_slice_in_dim(kvp,head*ROWS,ROWS,0)
    line=spread(copies(piece,LONG),"z").reshape(-1,2*D)
    near=spread(copies(line,CORE_CHIPS),PLANE).reshape(-1,2*D)
    far=swap(near)
    op,our,carry,own=run_forward(lengths,qp,gp,near,far,qr,gr,kvr)
    met=lax.ppermute(own[1].astype(jnp.float16),"x_lo",[(0,1),(1,0)])
    carry,dfar=run_backward(False,qp,gp,far,qr,gr,carry)
    carry,dfar,met=lax.optimization_barrier((carry,dfar,met))
    own=(unpack(own[0])+unpack(met)).reshape(LINES,-1,2*D)
    turns=[turn(own[i],i) for i in range(1,LINES)]
    dqr,dqp,chip=run_backward(True,qp,gp,near,qr,gr,carry,swap(dfar))
    chip,turns=lax.optimization_barrier((chip,turns))
    chip,own=lax.optimization_barrier((chip.astype(jnp.float16),own[0]+turns[0]+turns[1]+turns[2]))
    line=unpack(spread(chip,PLANE)).sum(0)
    strip=spread(line.reshape(LONG,ROWS,2*D),"z").sum(0)
    done=jnp.concatenate([strip,own]).astype(bf16)
    done=spread(copies(done,HEADS),HEAD)
    mine=done[:,ROWS:].reshape(LINES,2,-1,2*D).transpose(1,0,2,3).reshape(-1,2*D)
    return (op,our,dqp,dqr,done[:,:ROWS].reshape(-1,2*D),mine)

def solution(mesh):
    P=jax.sharding.PartitionSpec
    fine=jax.sharding.Mesh(mesh.devices.reshape(2,LONG,2,4,2),SEQ+HEAD)
    rows_,cache=P(SEQ,HEAD),P(SEQ,None)
    return jax.shard_map(on_device,mesh=fine,
        in_specs=(rows_,cache,rows_,cache,rows_,rows_,P(SEQ)),
        out_specs=(rows_,rows_,rows_,rows_,cache,cache),check_vma=False)
```

```python
import functools, math
import jax, jax.numpy as jnp
from jax import lax
from jax.experimental import pallas as pl
from jax.experimental.pallas import tpu as pltpu
f32=jnp.float32; bf16=jnp.bfloat16
D=128
SCALE=1.0/math.sqrt(D)
RATE=math.log2(math.e)*SCALE
FAR=1e30
OWN=256
SEQ=("x_hi","z","core")
HEAD=("y","x_lo")
PLANE=("x_hi","y","x_lo")
LONG=8
HEADS=8
LINES=4
TILE=8
CORE_CHIPS=16
ROWS=16

def dot(a,b): return jnp.dot(a,b,preferred_element_type=f32)
def flip(x): return x.astype(f32).T.astype(bf16)
def fold(x): return x.reshape(x.shape[0]//8,8,x.shape[1])
def rows(i,n): return pl.ds(i*n,n)
def loop(n,step,init):
    for i in range(n): init=step(i,init)
    return init

def key_place(core,start,n,share,strip):
    r=start+lax.broadcasted_iota(jnp.int32,(n,share),0)
    wide=lambda size: size.bit_length()-1
    x=r>>wide(strip*CORE_CHIPS//2); head=(r>>wide(strip))&(HEADS-1); z=(r>>wide(ROWS))&(LONG-1); t=r&(ROWS-1)
    return ((x*LONG+z)*2+core)*share+head*ROWS+t

def pack(ref,b,cols,x):
    n=x.shape[0]
    power=jnp.ceil(jnp.log2(jnp.maximum(jnp.max(jnp.abs(x),axis=0,keepdims=True),2.0**-100)))
    ref[*b,:n,cols]=x*jnp.exp2(-power)
    ref[*b,n:,cols]=jnp.broadcast_to(power,(TILE,x.shape[1]))

KEYS,VALUES=slice(0,D),slice(D,2*D)

def seq_place():
    return (lax.axis_index(SEQ[0])*LONG+lax.axis_index(SEQ[1]))*2+lax.axis_index(SEQ[2])

def forward(KC,info,qp,gp,near,far,qr,gr,kvr,op,our,carry,own2,enear,efar,own):
    length=info[0]; first=seq_place()*qp.shape[0]
    core=lax.axis_index("core")
    half=near.shape[0]; count=2*half; span=qr.shape[0]; share=qp.shape[0]; n=span+share
    qt=jnp.concatenate([flip(qr[...]),flip(qp[...])],axis=1)
    gt=jnp.concatenate([flip(gr[...]),flip(gp[...])],axis=1)
    def part(i):
        return (near if i*KC<half else far)[pl.ds(i*KC%half,KC),:]
    def scores(i):
        return (enear if i*KC<half else efar).at[pl.ds(i*KC%half,KC),:]
    def seen(i):
        place=key_place(core if i*KC<half else 1-core,i*KC%half,KC,share,half//CORE_CHIPS)
        return place<=first+lax.broadcasted_iota(jnp.int32,(KC,share),1)
    tri=lax.broadcasted_iota(jnp.int32,(OWN,OWN),0)<=lax.broadcasted_iota(jnp.int32,(OWN,OWN),1)
    def top(i,m):
        x=dot(part(i)[:,:D],qt)
        x=jnp.concatenate([x[:,:span],jnp.where(seen(i),x[:,span:],-FAR)],axis=1)
        scores(i)[...]=x
        return jnp.maximum(m,jnp.max(fold(x),axis=0))
    m=loop(count//KC,top,jnp.full((8,n),-FAR,f32))
    mr=m[:,:span]
    for j in range(span//OWN):
        x=dot(kvr[j*OWN:(j+1)*OWN,:D],qt[:,j*OWN:span])
        d=jnp.where(tri,x[:,:OWN],-FAR)
        x=d if x.shape[1]==OWN else jnp.concatenate([d,x[:,OWN:]],axis=1)
        own[j*OWN:(j+1)*OWN,j*OWN:span]=x
        y=jnp.max(fold(x),axis=0)
        y=jnp.maximum(mr[:,j*OWN:],y)
        mr=y if j==0 else jnp.concatenate([mr[:,:j*OWN],y],axis=1)
    m=jnp.max(jnp.concatenate([mr,m[:,span:]],axis=1),axis=0,keepdims=True)
    def total(i,l):
        e=jnp.exp2((scores(i)[...]-m)*RATE)
        scores(i)[...]=e
        return l+jnp.sum(fold(e),axis=0)
    l=loop(count//KC,total,jnp.zeros((8,n),f32))
    lr=l[:,:span]
    for j in range(span//OWN):
        e=jnp.exp2((own[j*OWN:(j+1)*OWN,j*OWN:span]-m[:,j*OWN:span])*RATE)
        own[j*OWN:(j+1)*OWN,j*OWN:span]=e
        y=lr[:,j*OWN:]+jnp.sum(fold(e),axis=0)
        lr=y if j==0 else jnp.concatenate([lr[:,:j*OWN],y],axis=1)
    l=jnp.sum(jnp.concatenate([lr,l[:,span:]],axis=1),axis=0,keepdims=True)
    at=lax.broadcasted_iota(jnp.int32,(1,n),1)
    live=(at<length)|(at>=span)
    inv=jnp.where(live,1.0/l,0.0)
    def attend(i,o):
        p=(scores(i)[...]*inv).astype(bf16)
        return o+dot(flip(part(i)[:,D:]),p)
    o=loop(count//KC,attend,jnp.zeros((D,n),f32))
    tail=o[:,span:]
    o=o[:,:span]
    for j in range(span//OWN):
        p=(own[j*OWN:(j+1)*OWN,j*OWN:span]*inv[:,j*OWN:span]).astype(bf16)
        y=o[:,j*OWN:]+dot(flip(kvr[j*OWN:(j+1)*OWN,D:]),p)
        o=y if j==0 else jnp.concatenate([o[:,:j*OWN],y],axis=1)
    our[...]=o.T.astype(bf16)
    op[...]=tail.T.astype(bf16)
    delta=jnp.sum(gt.astype(f32)*jnp.concatenate([o,tail],axis=1),axis=0,keepdims=True)
    carry[D:D+8,:]=jnp.broadcast_to(inv,(8,n))
    carry[D+8:,:]=jnp.broadcast_to(delta,(8,n))
    dq=jnp.zeros((D,span),f32)
    for j in range(span//OWN):
        a=slice(j*OWN,(j+1)*OWN); b=slice(j*OWN,span)
        p=own[a,b]*inv[:,b]
        dp=dot(kvr[a,D:],gt[:,b])
        ds=(p*(dp-delta[:,b])).astype(bf16)
        dv=dot(p.astype(bf16),gr[b,:])
        dk=dot(ds,qr[b,:])*SCALE
        strip=span//HEADS
        for t in range(OWN//strip):
            u=slice(t*strip,(t+1)*strip)
            x,y=divmod(j*(OWN//strip)+t,LINES)
            at=((y-lax.axis_index("y"))&(LINES-1),x^lax.axis_index("x_lo"))
            pack(own2,at,VALUES,dv[u])
            pack(own2,at,KEYS,dk[u])
        y=dq[:,b]+dot(flip(kvr[a,:D]),ds)
        dq=y if j==0 else jnp.concatenate([dq[:,:j*OWN],y],axis=1)
    carry[:D,:]=jnp.concatenate([dq,jnp.zeros((D,share),f32)],axis=1)

def combine(mine,other,out):
    n=mine.shape[0]//CORE_CHIPS
    for b in range(CORE_CHIPS):
        x=mine[rows(b,n),:]+other[rows(b,n),:]
        pack(out,(b,),slice(0,2*D),x)

def backward(KC,last,qp,gp,kv,qr,gr,e,carry,*out):
    *out,grad=out
    half=kv.shape[0]; span=qr.shape[0]; share=qp.shape[0]
    gt=jnp.concatenate([flip(gr[...]),flip(gp[...])],axis=1)
    q=jnp.concatenate([qr[...],qp[...]],axis=0)
    g=jnp.concatenate([gr[...],gp[...]],axis=0)
    inv=carry[D:D+1,:]; delta=carry[D+8:D+9,:]
    def step(i,dq):
        a=rows(i,KC)
        dp=dot(kv[a,D:],gt)
        p=e[a,:]*inv
        ds=(p*(dp-delta)).astype(bf16)
        dv=dot(p.astype(bf16),g)
        dk=dot(ds,q)*SCALE
        grad[a,D:]=dv
        grad[a,:D]=dk
        return dq+dot(flip(kv[a,:D]),ds)
    dq=loop(half//KC,step,carry[:D,:])
    if not last:
        out[0][:D,:]=dq
        out[0][D:,:]=carry[D:,:]
    else:
        dq=(dq*SCALE).T.astype(bf16)
        out[0][...]=dq[:span]
        out[1][...]=dq[span:]

V=pl.BlockSpec(memory_space=pltpu.VMEM)
SM=pl.BlockSpec(memory_space=pltpu.SMEM)
def shape(s,t=f32): return jax.ShapeDtypeStruct(s,t)

def run_forward(lengths,qp,gp,near,far,qr,gr,kvr,KC=512):
    span=qr.shape[0]; half=near.shape[0]; share=qp.shape[0]; n=span+share
    return pl.pallas_call(functools.partial(forward,KC),
        out_shape=(shape(qp.shape,bf16),shape(qr.shape,bf16),shape((D+16,n)),shape((LINES,2,span//HEADS+TILE,2*D)),shape((half,n)),shape((half,n))),
        in_specs=[SM]+[V]*7,out_specs=(V,)*6,
        scratch_shapes=[pltpu.VMEM((span,span),f32)],
        cost_estimate=pl.CostEstimate(flops=5*n*half*2*D,bytes_accessed=2**23,transcendentals=4*n*half),
        compiler_params=pltpu.CompilerParams(vmem_limit_bytes=22*1024*1024),name="forward")(lengths,qp,gp,near,far,qr,gr,kvr)

def run_backward(last,qp,gp,kv,qr,gr,e,carry,KC=512):
    n=carry.shape[1]; half=kv.shape[0]
    return pl.pallas_call(functools.partial(backward,KC,last),
        out_shape=((shape(qr.shape,bf16),shape(qp.shape,bf16)) if last else (shape(carry.shape),))+(shape(kv.shape),),
        in_specs=[V]*7,out_specs=(V,)*(2+last),
        cost_estimate=pl.CostEstimate(flops=50*n*half*2*D,bytes_accessed=2**22,transcendentals=n*half),
        compiler_params=pltpu.CompilerParams(vmem_limit_bytes=28*1024*1024),name="backward")(qp,gp,kv,qr,gr,e,carry)

def run_combine(mine,other):
    n=mine.shape[0]//CORE_CHIPS
    return pl.pallas_call(combine,out_shape=shape((CORE_CHIPS,n+TILE,2*D)),in_specs=[V]*2,out_specs=V,
        compiler_params=pltpu.CompilerParams(vmem_limit_bytes=16*1024*1024),name="combine")(mine,other)

def swap(x): return lax.ppermute(x,"core",[(0,1),(1,0)])
def spread(x,axes): return lax.all_to_all(x,axes,0,0,tiled=True)
def copies(x,n): return jnp.broadcast_to(x[None],(n,)+x.shape)

def unpack(x):
    rest=jnp.exp2(x[:,-TILE:].astype(f32))
    x=x[:,:-TILE].astype(f32).reshape(x.shape[0],-1,TILE,x.shape[2])
    return x*rest[:,None]

def turn(x,by): return lax.ppermute(x,"y",[(i,(i+by)%LINES) for i in range(LINES)])

def on_device(qp,kvp,qr,kvr,gp,gr,lengths):
    head=lax.axis_index(HEAD)
    piece=lax.dynamic_slice_in_dim(kvp,head*ROWS,ROWS,0)
    line=spread(copies(piece,LONG),"z").reshape(-1,2*D)
    near=spread(copies(line,CORE_CHIPS),PLANE).reshape(-1,2*D)
    far=swap(near)
    op,our,carry,own,enear,efar=run_forward(lengths,qp,gp,near,far,qr,gr,kvr)
    turns=[turn(own[i].astype(jnp.float16),i) for i in range(1,LINES)]
    carry,dfar=run_backward(False,qp,gp,far,qr,gr,efar,carry)
    recv=swap(dfar)
    carry,turns=lax.optimization_barrier((carry,turns))
    own=sum([unpack(x) for x in turns],unpack(own[0])).reshape(2,-1,2*D)
    met=lax.ppermute(own[1],"x_lo",[(0,1),(1,0)])
    dqr,dqp,dnear=run_backward(True,qp,gp,near,qr,gr,enear,carry)
    chip=run_combine(dnear,recv)
    chip,met=lax.optimization_barrier((chip,met))
    chip,own=lax.optimization_barrier((chip.astype(jnp.float16),own[0]+met))
    line=unpack(spread(chip,PLANE)).sum(0)
    strip=spread(line.reshape(LONG,ROWS,2*D),"z").sum(0)
    done=jnp.concatenate([strip,own]).astype(bf16)
    done=spread(copies(done,HEADS),HEAD)
    mine=done[:,ROWS:].reshape(LINES,2,-1,2*D).transpose(1,0,2,3).reshape(-1,2*D)
    return (op,our,dqp,dqr,done[:,:ROWS].reshape(-1,2*D),mine)

def solution(mesh):
    P=jax.sharding.PartitionSpec
    fine=jax.sharding.Mesh(mesh.devices.reshape(2,LONG,2,4,2),SEQ+HEAD)
    rows_,cache=P(SEQ,HEAD),P(SEQ,None)
    return jax.shard_map(on_device,mesh=fine,
        in_specs=(rows_,cache,rows_,cache,rows_,rows_,P(SEQ)),
        out_specs=(rows_,rows_,rows_,rows_,cache,cache),check_vma=False)
```

```python
import functools, math
import jax, jax.numpy as jnp
from jax import lax
from jax.experimental import pallas as pl
from jax.experimental.pallas import tpu as pltpu
f32=jnp.float32; bf16=jnp.bfloat16
D=128
SCALE=1.0/math.sqrt(D)
RATE=math.log2(math.e)*SCALE
FAR=1e30
OWN=256
EARLY=512
SEQ=("x_hi","z","core")
HEAD=("y","x_lo")
PLANE=("x_hi","y","x_lo")
LONG=8
HEADS=8
LINES=4
TILE=8
CORE_CHIPS=16
ROWS=16

def dot(a,b): return jnp.dot(a,b,preferred_element_type=f32)
def flip(x): return x.T
def fold(x): return x.reshape(x.shape[0]//8,8,x.shape[1])
def rows(i,n): return pl.ds(i*n,n)
def loop(n,step,init):
    for i in range(n): init=step(i,init)
    return init

def key_place(core,start,n,share,strip):
    r=start+lax.broadcasted_iota(jnp.int32,(n,share),0)
    wide=lambda size: size.bit_length()-1
    x=r>>wide(strip*CORE_CHIPS//2); head=(r>>wide(strip))&(HEADS-1); z=(r>>wide(ROWS))&(LONG-1); t=r&(ROWS-1)
    return ((x*LONG+z)*2+core)*share+head*ROWS+t

def pack(ref,b,cols,x):
    n=x.shape[0]
    power=jnp.ceil(jnp.log2(jnp.maximum(jnp.max(jnp.abs(x),axis=0,keepdims=True),2.0**-100)))
    ref[*b,:n,cols]=x*jnp.exp2(-power)
    ref[*b,n:,cols]=jnp.broadcast_to(power,(TILE,x.shape[1]))

KEYS,VALUES=slice(0,D),slice(D,2*D)

def seq_place():
    return (lax.axis_index(SEQ[0])*LONG+lax.axis_index(SEQ[1]))*2+lax.axis_index(SEQ[2])

def forward(KC,info,qp,gp,near,far,qr,gr,kvr,op,our,carry,own2,enear,efar,own):
    length=info[0]; first=seq_place()*qp.shape[0]
    core=lax.axis_index("core")
    half=near.shape[0]; count=2*half; span=qr.shape[0]; share=qp.shape[0]; n=span+share
    qt=jnp.concatenate([flip(qr[...]),flip(qp[...])],axis=1)
    gt=jnp.concatenate([flip(gr[...]),flip(gp[...])],axis=1)
    def part(i):
        return (near if i*KC<half else far)[pl.ds(i*KC%half,KC),:]
    def scores(i):
        return (enear if i*KC<half else efar).at[pl.ds(i*KC%half,KC),:]
    def seen(i):
        place=key_place(core if i*KC<half else 1-core,i*KC%half,KC,share,half//CORE_CHIPS)
        return place<=first+lax.broadcasted_iota(jnp.int32,(KC,share),1)
    tri=lax.broadcasted_iota(jnp.int32,(OWN,OWN),0)<=lax.broadcasted_iota(jnp.int32,(OWN,OWN),1)
    def top(i,m):
        x=dot(part(i)[:,:D],qt)
        x=jnp.concatenate([x[:,:span],jnp.where(seen(i),x[:,span:],-FAR)],axis=1)
        scores(i)[...]=x
        return jnp.maximum(m,jnp.max(fold(x),axis=0))
    m=loop(count//KC,top,jnp.full((8,n),-FAR,f32))
    mr=m[:,:span]
    for j in range(span//OWN):
        x=dot(kvr[j*OWN:(j+1)*OWN,:D],qt[:,j*OWN:span])
        d=jnp.where(tri,x[:,:OWN],-FAR)
        x=d if x.shape[1]==OWN else jnp.concatenate([d,x[:,OWN:]],axis=1)
        own[j*OWN:(j+1)*OWN,j*OWN:span]=x
        y=jnp.max(fold(x),axis=0)
        y=jnp.maximum(mr[:,j*OWN:],y)
        mr=y if j==0 else jnp.concatenate([mr[:,:j*OWN],y],axis=1)
    m=jnp.max(jnp.concatenate([mr,m[:,span:]],axis=1),axis=0,keepdims=True)
    def total(i,l):
        e=jnp.exp2((scores(i)[...]-m)*RATE)
        scores(i)[...]=e
        return l+jnp.sum(fold(e),axis=0)
    l=loop(count//KC,total,jnp.zeros((8,n),f32))
    lr=l[:,:span]
    for j in range(span//OWN):
        e=jnp.exp2((own[j*OWN:(j+1)*OWN,j*OWN:span]-m[:,j*OWN:span])*RATE)
        own[j*OWN:(j+1)*OWN,j*OWN:span]=e
        y=lr[:,j*OWN:]+jnp.sum(fold(e),axis=0)
        lr=y if j==0 else jnp.concatenate([lr[:,:j*OWN],y],axis=1)
    l=jnp.sum(jnp.concatenate([lr,l[:,span:]],axis=1),axis=0,keepdims=True)
    at=lax.broadcasted_iota(jnp.int32,(1,n),1)
    live=(at<length)|(at>=span)
    inv=jnp.where(live,1.0/l,0.0)
    def attend(i,o):
        p=(scores(i)[...]*inv).astype(bf16)
        return o+dot(flip(part(i)[:,D:]),p)
    o=loop(count//KC,attend,jnp.zeros((D,n),f32))
    tail=o[:,span:]
    o=o[:,:span]
    for j in range(span//OWN):
        p=(own[j*OWN:(j+1)*OWN,j*OWN:span]*inv[:,j*OWN:span]).astype(bf16)
        y=o[:,j*OWN:]+dot(flip(kvr[j*OWN:(j+1)*OWN,D:]),p)
        o=y if j==0 else jnp.concatenate([o[:,:j*OWN],y],axis=1)
    our[...]=o.T.astype(bf16)
    op[...]=tail.T.astype(bf16)
    delta=jnp.sum(gt.astype(f32)*jnp.concatenate([o,tail],axis=1),axis=0,keepdims=True)
    carry[D:D+8,:]=jnp.broadcast_to(inv,(8,n))
    carry[D+8:,:]=jnp.broadcast_to(delta,(8,n))
    dq=jnp.zeros((D,span),f32)
    for j in range(span//OWN):
        a=slice(j*OWN,(j+1)*OWN); b=slice(j*OWN,span)
        p=own[a,b]*inv[:,b]
        dp=dot(kvr[a,D:],gt[:,b])
        ds=(p*(dp-delta[:,b])).astype(bf16)
        dv=dot(p.astype(bf16),gr[b,:])
        dk=dot(ds,qr[b,:])*SCALE
        strip=span//HEADS
        for t in range(OWN//strip):
            u=slice(t*strip,(t+1)*strip)
            x,y=divmod(j*(OWN//strip)+t,LINES)
            at=((y-lax.axis_index("y"))&(LINES-1),x^lax.axis_index("x_lo"))
            pack(own2,at,VALUES,dv[u])
            pack(own2,at,KEYS,dk[u])
        y=dq[:,b]+dot(flip(kvr[a,:D]),ds)
        dq=y if j==0 else jnp.concatenate([dq[:,:j*OWN],y],axis=1)
    carry[:D,:]=jnp.concatenate([dq,jnp.zeros((D,share),f32)],axis=1)

def combine(first,rest,other,out):
    n=other.shape[0]//CORE_CHIPS
    for b in range(CORE_CHIPS):
        mine=first[rows(b,n),:] if b*n<EARLY else rest[pl.ds(b*n-EARLY,n),:]
        pack(out,(b,),slice(0,2*D),mine+other[rows(b,n),:])

def backward(KC,last,qp,gp,qr,gr,carry,near,enear,*out):
    half=near.shape[0]; span=qr.shape[0]; share=qp.shape[0]
    if last:
        *out,gnear=out
        work=[(near,enear,gnear,i,i-EARLY//KC) for i in range(EARLY//KC,half//KC)]
    else:
        far,efar,*out,gnear,gfar=out
        work=[(far,efar,gfar,i,i) for i in range(half//KC)]+[(near,enear,gnear,i,i) for i in range(EARLY//KC)]
    gt=jnp.concatenate([flip(gr[...]),flip(gp[...])],axis=1)
    q=jnp.concatenate([qr[...],qp[...]],axis=0)
    g=jnp.concatenate([gr[...],gp[...]],axis=0)
    inv=carry[D:D+1,:]; delta=carry[D+8:D+9,:]
    dq=carry[:D,:]
    for kv,e,grad,i,o in work:
        a=rows(i,KC)
        dp=dot(kv[a,D:],gt)
        p=e[a,:]*inv
        ds=(p*(dp-delta)).astype(bf16)
        grad[rows(o,KC),D:]=dot(p.astype(bf16),g)
        grad[rows(o,KC),:D]=dot(ds,q)*SCALE
        dq=dq+dot(flip(kv[a,:D]),ds)
    if not last:
        out[0][:D,:]=dq
        out[0][D:,:]=carry[D:,:]
    else:
        dq=(dq*SCALE).T.astype(bf16)
        out[0][...]=dq[:span]
        out[1][...]=dq[span:]

V=pl.BlockSpec(memory_space=pltpu.VMEM)
SM=pl.BlockSpec(memory_space=pltpu.SMEM)
def shape(s,t=f32): return jax.ShapeDtypeStruct(s,t)

def run_forward(lengths,qp,gp,near,far,qr,gr,kvr,KC=512):
    span=qr.shape[0]; half=near.shape[0]; share=qp.shape[0]; n=span+share
    return pl.pallas_call(functools.partial(forward,KC),
        out_shape=(shape(qp.shape,bf16),shape(qr.shape,bf16),shape((D+16,n)),shape((LINES,2,span//HEADS+TILE,2*D)),shape((half,n)),shape((half,n))),
        in_specs=[SM]+[V]*7,out_specs=(V,)*6,
        scratch_shapes=[pltpu.VMEM((span,span),f32)],
        cost_estimate=pl.CostEstimate(flops=5*n*half*2*D,bytes_accessed=2**23,transcendentals=4*n*half),
        compiler_params=pltpu.CompilerParams(vmem_limit_bytes=22*1024*1024),name="forward")(lengths,qp,gp,near,far,qr,gr,kvr)

def run_backward(last,qp,gp,qr,gr,carry,near,enear,*far,KC=512):
    n=carry.shape[1]; half=near.shape[0]
    if last:
        out=(shape(qr.shape,bf16),shape(qp.shape,bf16),shape((half-EARLY,2*D)))
    else:
        out=(shape(carry.shape),shape((EARLY,2*D)),shape(near.shape))
    return pl.pallas_call(functools.partial(backward,KC,last),
        out_shape=out,in_specs=[V]*(7+len(far)),out_specs=(V,)*3,
        cost_estimate=pl.CostEstimate(flops=50*n*half*2*D,bytes_accessed=2**22,transcendentals=n*half),
        compiler_params=pltpu.CompilerParams(vmem_limit_bytes=20*1024*1024),name="backward")(qp,gp,qr,gr,carry,near,enear,*far)

def run_combine(first,rest,other):
    n=other.shape[0]//CORE_CHIPS
    return pl.pallas_call(combine,out_shape=shape((CORE_CHIPS,n+TILE,2*D)),in_specs=[V]*3,out_specs=V,
        compiler_params=pltpu.CompilerParams(vmem_limit_bytes=16*1024*1024),name="combine")(first,rest,other)

def swap(x): return lax.ppermute(x,"core",[(0,1),(1,0)])
def spread(x,axes): return lax.all_to_all(x,axes,0,0,tiled=True)
def copies(x,n): return jnp.broadcast_to(x[None],(n,)+x.shape)

def unpack(x):
    rest=jnp.exp2(x[:,-TILE:].astype(f32))
    x=x[:,:-TILE].astype(f32).reshape(x.shape[0],-1,TILE,x.shape[2])
    return x*rest[:,None]

def turn(x,by): return lax.ppermute(x,"y",[(i,(i+by)%LINES) for i in range(LINES)])

def on_device(qp,kvp,qr,kvr,gp,gr,lengths):
    head=lax.axis_index(HEAD)
    piece=lax.dynamic_slice_in_dim(kvp,head*ROWS,ROWS,0)
    line=spread(copies(piece,LONG),"z").reshape(-1,2*D)
    near=spread(copies(line,CORE_CHIPS),PLANE).reshape(-1,2*D)
    far=swap(near)
    op,our,carry,own,enear,efar=run_forward(lengths,qp,gp,near,far,qr,gr,kvr)
    turns=[turn(own[i].astype(jnp.float16),i) for i in range(1,LINES)]
    carry,dearly,dfar=run_backward(False,qp,gp,qr,gr,carry,near,enear,far,efar)
    recv=swap(dfar)
    carry,turns=lax.optimization_barrier((carry,turns))
    own=sum([unpack(x) for x in turns],unpack(own[0])).reshape(2,-1,2*D)
    met=lax.ppermute(own[1],"x_lo",[(0,1),(1,0)])
    dqr,dqp,dnear=run_backward(True,qp,gp,qr,gr,carry,near,enear)
    chip=run_combine(dearly,dnear,recv)
    chip,met=lax.optimization_barrier((chip,met))
    chip,own=lax.optimization_barrier((chip.astype(jnp.float16),own[0]+met))
    line=unpack(spread(chip,PLANE)).sum(0)
    strip=spread(line.reshape(LONG,ROWS,2*D),"z").sum(0)
    done=jnp.concatenate([strip,own]).astype(bf16)
    done=spread(copies(done,HEADS),HEAD)
    mine=done[:,ROWS:].reshape(LINES,2,-1,2*D).transpose(1,0,2,3).reshape(-1,2*D)
    return (op,our,dqp,dqr,done[:,:ROWS].reshape(-1,2*D),mine)

def solution(mesh):
    P=jax.sharding.PartitionSpec
    fine=jax.sharding.Mesh(mesh.devices.reshape(2,LONG,2,4,2),SEQ+HEAD)
    rows_,cache=P(SEQ,HEAD),P(SEQ,None)
    return jax.shard_map(on_device,mesh=fine,
        in_specs=(rows_,cache,rows_,cache,rows_,rows_,P(SEQ)),
        out_specs=(rows_,rows_,rows_,rows_,cache,cache),check_vma=False)
```
